32 devices in a mesh: row: 4 (over z), col: 8 (over y, x, core).
Axes of the slice: x: 2, y: 2, z: 4, core: 2. Of those that a mesh axis runs over, the one named last changes fastest.
Arguments:
- inputs: bfloat16 [128, 12288], P('col', 'row'), may hold values from -6 to 6
- out_grad: bfloat16 [128, 12288], P('col', 'row'), may hold values from -5 to 5
- weight_in: bfloat16 [12288, 24576], P('row', 'col'), may hold values from -0.0546875 to 0.0546875
- weight_out: bfloat16 [24576, 12288], P('col', 'row'), may hold values from -0.0390625 to 0.0390625
Outputs:
- grad_input: bfloat16 [128, 12288], P('col', 'row')
- grad_weight_in: bfloat16 [12288, 24576], P('row', 'col')
- grad_weight_out: bfloat16 [24576, 12288], P('col', 'row')
The draws below stay inside these ranges and needn't reach their ends.
All inputs are finite; a program needn't handle non-finite values.
Results may differ from the reference program's by a relative error of at most 0.0049.
Values may be sent and summed in bfloat16 or wider, within the bound.
A program may use at most 128 MiB of HBM per device.

```python
import jax
import jax.numpy as jnp
from jax import lax

D = 12288
FF = 24576
TOKENS = 128


def block_levels(key, shape, cuts, low, high):
    loudness = 1.0
    for axis_at, parts in cuts:
        steps = jax.random.uniform(jax.random.fold_in(jax.random.fold_in(key, 6), axis_at), (parts,), jnp.float32, low / len(cuts), high / len(cuts))
        loudness = loudness * jnp.repeat(jnp.exp(steps), shape[axis_at] // parts).reshape((-1,) + (1,) * (len(shape) - 1 - axis_at))
    return loudness


def noise(stream_key, dims, scale, most, split=(), kind=jnp.bfloat16):
    entries = scale * jax.random.normal(stream_key, dims, jnp.float32)
    if split:
        entries = entries * block_levels(stream_key, dims, split, -0.22, 0.18)
    return jnp.clip(entries, -most, most).astype(kind)


def setup_inputs(seed: int = 0) -> dict:
    arg_keys = jax.random.split(jax.random.key(seed), 5)
    inputs = noise(arg_keys[0], (TOKENS, D), 1.0, 6.0, ((0, 8), (1, 4)))
    out_grad = noise(arg_keys[1], (TOKENS, D), (4.0 / TOKENS ** 0.5), 5.0, ((0, 8), (1, 4)))
    weight_in = noise(arg_keys[2], (D, FF), D ** -0.5, 0.0546875, ((0, 4), (1, 8)))
    weight_out = noise(arg_keys[3], (FF, D), FF ** -0.5, 0.0390625, ((0, 8), (1, 4)))
    return dict(inputs=inputs, out_grad=out_grad, weight_in=weight_in, weight_out=weight_out)


gelu_cubic = 0.044715
root_two_pi = 0.7978845608028654


def reference(inputs, out_grad, weight_in, weight_out):
    preact = jnp.dot(inputs, weight_in, preferred_element_type=jnp.float32)
    act_grad = lax.dot_general(out_grad, weight_out, (((1,), (1,)), ((), ())), preferred_element_type=jnp.float32)
    inner = root_two_pi * (preact + gelu_cubic * preact * preact * preact)
    tangent = jnp.tanh(inner)
    hidden = (0.5 * preact * (1.0 + tangent)).astype(jnp.bfloat16)
    slope = 0.5 * (1.0 + tangent) + 0.5 * preact * (1.0 - tangent * tangent) * root_two_pi * (1.0 + 3.0 * gelu_cubic * preact * preact)
    hid_grad = (act_grad * slope).astype(jnp.bfloat16)
    grad_weight_out = lax.dot_general(hidden, out_grad, (((0,), (0,)), ((), ())), preferred_element_type=jnp.float32).astype(jnp.bfloat16)
    grad_weight_in = lax.dot_general(inputs, hid_grad, (((0,), (0,)), ((), ())), preferred_element_type=jnp.float32).astype(jnp.bfloat16)
    grad_input = lax.dot_general(hid_grad, weight_in, (((1,), (1,)), ((), ())), preferred_element_type=jnp.float32).astype(jnp.bfloat16)
    return grad_input, grad_weight_in, grad_weight_out
```

```python
import functools

import jax
import jax.numpy as jnp
from jax import lax
from jax.experimental import pallas as pl
from jax.experimental.pallas import tpu as pltpu
from jax.sharding import PartitionSpec as P

gelu_cubic = 0.044715
root_two_pi = 0.7978845608028654
MESH = pl.DeviceIdType.MESH
bf16, f32 = jnp.bfloat16, jnp.float32


def gelu_pair(preact, act_grad):
    inner = root_two_pi * (preact + gelu_cubic * preact * preact * preact)
    tangent = jnp.tanh(inner)
    hidden = (0.5 * preact * (1.0 + tangent)).astype(bf16)
    slope = 0.5 * (1.0 + tangent) + 0.5 * preact * (1.0 - tangent * tangent) * root_two_pi * (
        1.0 + 3.0 * gelu_cubic * preact * preact
    )
    hid_grad = (act_grad * slope).astype(bf16)
    return (hidden, hid_grad)


def nt_dot(a, b):
    return lax.dot_general(a, b, (((1,), (1,)), ((), ())), preferred_element_type=f32)


def tn_dot(a, b):
    return lax.dot_general(a, b, (((0,), (0,)), ((), ())), preferred_element_type=f32)


def exchange_kernel(
    n_row, n_col, nch, fc,
    x_ref, g_ref, win_ref, wout_ref,
    h_out, x_out, g_out, gi_out,
    xf, gf, wi, wo, s, r, e, hb, keep, pf, gi,
    w_sem, ag_send, ag_recv, own_sem, s_send, s_recv, e_send, e_recv, h_send, h_recv, out_sem,
):
    row, col = lax.axis_index("row"), lax.axis_index("col")
    core, chip = lax.rem(col, 2), col // 2
    chips = n_col // 2
    rows = x_ref.shape[0]
    half_n = n_row // 2
    side = (row >= half_n).astype(jnp.int32)
    other = 1 - side
    place = jnp.where(side == 0, row, n_row - 1 - row)
    inner = jnp.where(side == 0, row + 1, row - 1)
    outer = jnp.where(side == 0, jnp.maximum(row - 1, 0), jnp.minimum(row + 1, n_row - 1))
    has_out = place > 0
    is_mid = place == half_n - 1

    def weight_in(c):
        return pltpu.make_async_copy(
            win_ref.at[:, pl.ds(pl.multiple_of(c * fc, fc), fc)], wi.at[c], w_sem.at[0, c]
        )

    def weight_out(c):
        return pltpu.make_async_copy(
            wout_ref.at[pl.ds(pl.multiple_of(c * fc, fc), fc), :], wo.at[c], w_sem.at[1, c]
        )

    def mine(k):
        src, dst = ((x_ref, xf), (g_ref, gf))[k]
        return pltpu.make_async_copy(src, dst.at[pl.ds(pl.multiple_of(col * rows, rows), rows), :], own_sem.at[k])

    for k in range(2):
        mine(k).start()

    def fetch(c, carry):
        weight_in(c).start()
        weight_out(c).start()
        return carry

    lax.fori_loop(0, nch, fetch, 0)

    barrier = pltpu.get_barrier_semaphore()
    for q in range(1, chips):
        pl.semaphore_signal(
            barrier, inc=1, device_id={"col": lax.rem(chip + q, chips) * 2 + core}, device_id_type=MESH
        )
    pl.semaphore_signal(barrier, inc=1, device_id={"col": chip * 2 + 1 - core}, device_id_type=MESH)
    pl.semaphore_signal(barrier, inc=1, device_id={"row": inner}, device_id_type=MESH)

    @pl.when(has_out)
    def _():
        pl.semaphore_signal(barrier, inc=1, device_id={"row": outer}, device_id_type=MESH)

    pl.semaphore_wait(barrier, chips + 1 + has_out.astype(jnp.int32))

    def block(k, owner):
        return (xf, gf)[k].at[pl.ds(pl.multiple_of(owner * rows, rows), rows), :]

    def far(k, q):
        return pltpu.make_async_remote_copy(
            src_ref=(x_ref, g_ref)[k],
            dst_ref=block(k, col),
            send_sem=ag_send.at[k, q],
            recv_sem=ag_recv.at[k, col],
            device_id={"col": lax.rem(chip + q, chips) * 2 + core},
            device_id_type=MESH,
        )

    def near(k, q):
        owner = lax.rem(chip + chips - q, chips) * 2 + core
        return pltpu.make_async_remote_copy(
            src_ref=x_ref if (q == 0 and k == 0) else g_ref if q == 0 else block(k, owner),
            dst_ref=block(k, owner),
            send_sem=ag_send.at[k, chips + q],
            recv_sem=ag_recv.at[k, owner],
            device_id={"col": chip * 2 + 1 - core},
            device_id_type=MESH,
        )

    def landed(k, owner):
        return pltpu.make_async_remote_copy(
            src_ref=block(k, owner),
            dst_ref=block(k, owner),
            send_sem=ag_send.at[k, 0],
            recv_sem=ag_recv.at[k, owner],
            device_id={"col": chip * 2 + 1 - core},
            device_id_type=MESH,
        )

    for k in range(2):
        for q in range(1, chips):
            far(k, q).start()
        near(k, 0).start()
    for k in range(2):
        mine(k).wait()
        for q in range(1, chips):
            landed(k, lax.rem(chip + chips - q, chips) * 2 + core).wait_recv()
            near(k, q).start()
    for k in range(2):
        for q in range(chips):
            landed(k, lax.rem(chip + chips - q, chips) * 2 + 1 - core).wait_recv()
    pltpu.make_async_copy(xf, x_out, out_sem.at[0]).start()
    pltpu.make_async_copy(gf, g_out, out_sem.at[1]).start()

    gi[...] = jnp.zeros_like(gi)

    def send_sum(c):
        return pltpu.make_async_remote_copy(
            src_ref=s.at[c], dst_ref=r.at[c], send_sem=s_send.at[c], recv_sem=s_recv.at[c],
            device_id={"row": inner}, device_id_type=MESH,
        )

    def swap_sum(c):
        return pltpu.make_async_remote_copy(
            src_ref=s.at[c, other], dst_ref=e.at[c], send_sem=e_send.at[c], recv_sem=e_recv.at[c],
            device_id={"row": inner}, device_id_type=MESH,
        )

    def send_hidden(c, half, target, way):
        return pltpu.make_async_remote_copy(
            src_ref=hb.at[c, half], dst_ref=hb.at[c, half],
            send_sem=h_send.at[c, half, way], recv_sem=h_recv.at[c, half],
            device_id={"row": target}, device_id_type=MESH,
        )

    def save_hidden(c):
        return pltpu.make_async_copy(hb.at[c], h_out.at[c], out_sem.at[3 + c])

    tokens = xf.shape[0]
    split = tokens // 2

    def local_sums(c):
        weight_in(c).wait()
        weight_out(c).wait()
        pf[:, 0] = jnp.dot(xf[...], wi[c], preferred_element_type=f32).reshape(2, split, fc)
        pf[:, 1] = nt_dot(gf[...], wo[c]).reshape(2, split, fc)

        @pl.when(has_out)
        def _():
            send_sum(c).wait_recv()
            pf[...] += r[c].astype(f32)

    def input_terms(c):
        save_hidden(c).start()
        grads = hb[c, :, 1].reshape(tokens, fc)
        gi[...] += nt_dot(grads, wi[c])

    @pl.when(jnp.logical_not(is_mid))
    def _():
        def inwards(c, carry):
            local_sums(c)
            s[c] = pf[...].astype(bf16)
            send_sum(c).start()
            return carry

        lax.fori_loop(0, nch, inwards, 0)

        def outwards(c, carry):
            for half in range(2):
                send_hidden(c, half, inner, 0).wait_recv()

                @pl.when(has_out)
                def _():
                    send_hidden(c, half, outer, 1).start()

            input_terms(c)
            return carry

        lax.fori_loop(0, nch, outwards, 0)

        def drain(c, carry):
            send_sum(c).wait_send()

            @pl.when(has_out)
            def _():
                for half in range(2):
                    send_hidden(c, half, outer, 1).wait_send()

            return carry

        lax.fori_loop(0, nch, drain, 0)

    @pl.when(is_mid)
    def _():
        def tick(t, carry):
            @pl.when(t < nch)
            def _():
                local_sums(t)
                s[t, other] = pf[other].astype(bf16)
                swap_sum(t).start()
                keep[lax.rem(t, 2)] = pf[side]

            @pl.when((t >= 1) & (t <= nch))
            def _():
                c = t - 1
                swap_sum(c).wait_recv()
                both = keep[lax.rem(c, 2)] + e[c].astype(f32)
                hidden, hid_grad = gelu_pair(both[0], both[1])
                hb[c, side, 0] = hidden
                hb[c, side, 1] = hid_grad
                send_hidden(c, side, inner, 0).start()

                @pl.when(has_out)
                def _():
                    send_hidden(c, side, outer, 1).start()

            @pl.when(t >= 2)
            def _():
                c = t - 2
                send_hidden(c, other, inner, 0).wait_recv()

                @pl.when(has_out)
                def _():
                    send_hidden(c, other, outer, 1).start()

                input_terms(c)

            return carry

        lax.fori_loop(0, nch + 2, tick, 0)

        def drain(c, carry):
            swap_sum(c).wait_send()
            send_hidden(c, side, inner, 0).wait_send()

            @pl.when(has_out)
            def _():
                send_hidden(c, side, outer, 1).wait_send()
                send_hidden(c, other, outer, 1).wait_send()

            return carry

        lax.fori_loop(0, nch, drain, 0)

    last = pltpu.make_async_copy(gi, gi_out, out_sem.at[2])
    last.start()
    for k in range(2):
        for q in range(1, chips):
            far(k, q).wait_send()
        for q in range(chips):
            near(k, q).wait_send()
    pltpu.make_async_copy(xf, x_out, out_sem.at[0]).wait()
    pltpu.make_async_copy(gf, g_out, out_sem.at[1]).wait()

    def saved(c, carry):
        save_hidden(c).wait()
        return carry

    lax.fori_loop(0, nch, saved, 0)
    last.wait()


def weights_kernel(nch, fc, x_ref, g_ref, hid_ref, all_ref, gwi_ref, gwo_ref):
    tokens = g_ref.shape[0]
    gwo_ref[...] = tn_dot(hid_ref[0, :, 0].reshape(tokens, fc), g_ref[...]).astype(bf16)
    for c in range(nch):
        grads = all_ref[c, :, 1].reshape(tokens, fc)
        gwi_ref[:, c * fc : (c + 1) * fc] = tn_dot(x_ref[...], grads).astype(bf16)


def on_device(n_row, n_col, inputs, out_grad, weight_in, weight_out):
    rows, d = inputs.shape
    f = weight_in.shape[1]
    tokens = rows * n_col
    fc = 256 if f % 256 == 0 else 128
    nch = f // fc
    split = tokens // 2
    any_spec = pl.BlockSpec(memory_space=pl.ANY)
    dma = pltpu.SemaphoreType.DMA
    hid, full_in, full_grad, terms = pl.pallas_call(
        functools.partial(exchange_kernel, n_row, n_col, nch, fc),
        out_shape=(
            jax.ShapeDtypeStruct((nch, 2, 2, split, fc), bf16),
            jax.ShapeDtypeStruct((tokens, d), bf16),
            jax.ShapeDtypeStruct((tokens, d), bf16),
            jax.ShapeDtypeStruct((tokens, d), f32),
        ),
        in_specs=[any_spec] * 4,
        out_specs=(any_spec,) * 4,
        scratch_shapes=[
            pltpu.VMEM((tokens, d), bf16),
            pltpu.VMEM((tokens, d), bf16),
            pltpu.VMEM((nch, d, fc), bf16),
            pltpu.VMEM((nch, fc, d), bf16),
            pltpu.VMEM((nch, 2, 2, split, fc), bf16),
            pltpu.VMEM((nch, 2, 2, split, fc), bf16),
            pltpu.VMEM((nch, 2, split, fc), bf16),
            pltpu.VMEM((nch, 2, 2, split, fc), bf16),
            pltpu.VMEM((2, 2, split, fc), f32),
            pltpu.VMEM((2, 2, split, fc), f32),
            pltpu.VMEM((tokens, d), f32),
            dma((2, nch)),
            dma((2, n_col)),
            dma((2, n_col)),
            dma((2,)),
            dma((nch,)),
            dma((nch,)),
            dma((nch,)),
            dma((nch,)),
            dma((nch, 2, 2)),
            dma((nch, 2)),
            dma((3 + nch,)),
        ],
        compiler_params=pltpu.CompilerParams(
            collective_id=0, has_side_effects=True, vmem_limit_bytes=56 * 2**20
        ),
        cost_estimate=pl.CostEstimate(
            flops=6 * tokens * d * f, bytes_accessed=4 * d * f, transcendentals=tokens * f
        ),
        name="exchange",
    )(inputs, out_grad, weight_in, weight_out)

    wide = fc if d % nch else d // nch
    steps = nch
    grad_weight_in, grad_weight_out = pl.pallas_call(
        functools.partial(weights_kernel, nch, fc),
        grid=(steps,),
        out_shape=(jax.ShapeDtypeStruct((d, f), bf16), jax.ShapeDtypeStruct((f, d), bf16)),
        in_specs=[
            pl.BlockSpec((tokens, wide), lambda i: (0, i)),
            pl.BlockSpec((tokens, d), lambda i: (0, 0)),
            pl.BlockSpec((1, 2, 2, split, fc), lambda i: (i, 0, 0, 0, 0)),
            pl.BlockSpec((nch, 2, 2, split, fc), lambda i: (0, 0, 0, 0, 0)),
        ],
        out_specs=(
            pl.BlockSpec((wide, f), lambda i: (i, 0)),
            pl.BlockSpec((fc, d), lambda i: (i, 0)),
        ),
        compiler_params=pltpu.CompilerParams(vmem_limit_bytes=40 * 2**20),
        cost_estimate=pl.CostEstimate(
            flops=4 * tokens * d * f, bytes_accessed=4 * d * f, transcendentals=0
        ),
        name="weight_grads",
    )(full_in, full_grad, hid, hid)
    grad_input = lax.psum_scatter(terms, "col", scatter_dimension=0, tiled=True).astype(bf16)
    return (grad_input, grad_weight_in, grad_weight_out)


def solution(mesh):
    placed = (P("col", "row"), P("col", "row"), P("row", "col"), P("col", "row"))
    return jax.shard_map(
        functools.partial(on_device, mesh.shape["row"], mesh.shape["col"]),
        mesh=mesh,
        in_specs=placed,
        out_specs=(P("col", "row"), P("row", "col"), P("col", "row")),
        check_vma=False,
    )
```

```python
import functools

import jax
import jax.numpy as jnp
from jax import lax
from jax.experimental import pallas as pl
from jax.experimental.pallas import tpu as pltpu
from jax.sharding import PartitionSpec as P

gelu_cubic = 0.044715
root_two_pi = 0.7978845608028654
MESH = pl.DeviceIdType.MESH
bf16, f32 = jnp.bfloat16, jnp.float32


def gelu_pair(preact, act_grad):
    inner = root_two_pi * (preact + gelu_cubic * preact * preact * preact)
    tangent = jnp.tanh(inner)
    hidden = (0.5 * preact * (1.0 + tangent)).astype(bf16)
    slope = 0.5 * (1.0 + tangent) + 0.5 * preact * (1.0 - tangent * tangent) * root_two_pi * (
        1.0 + 3.0 * gelu_cubic * preact * preact
    )
    hid_grad = (act_grad * slope).astype(bf16)
    return (hidden, hid_grad)


def nt_dot(a, b):
    return lax.dot_general(a, b, (((1,), (1,)), ((), ())), preferred_element_type=f32)


def tn_dot(a, b):
    return lax.dot_general(a, b, (((0,), (0,)), ((), ())), preferred_element_type=f32)


def exchange_kernel(
    n_row, n_col, nch, fc,
    x_ref, g_ref, win_ref, wout_ref,
    h_out, x_out, g_out, gi_out,
    xf, gf, wi, wo, s, r, e, hb, keep, pf, gi, pair, part, came, result,
    w_sem, ag_send, ag_recv, own_sem, s_send, s_recv, e_send, e_recv, h_send, h_recv, out_sem,
    pair_send, pair_recv, part_send, part_recv,
):
    row, col = lax.axis_index("row"), lax.axis_index("col")
    core, chip = lax.rem(col, 2), col // 2
    chips = n_col // 2
    rows = x_ref.shape[0]
    half_n = n_row // 2
    side = (row >= half_n).astype(jnp.int32)
    other = 1 - side
    place = jnp.where(side == 0, row, n_row - 1 - row)
    inner = jnp.where(side == 0, row + 1, row - 1)
    outer = jnp.where(side == 0, jnp.maximum(row - 1, 0), jnp.minimum(row + 1, n_row - 1))
    has_out = place > 0
    is_mid = place == half_n - 1

    def weight_in(c):
        return pltpu.make_async_copy(
            win_ref.at[:, pl.ds(pl.multiple_of(c * fc, fc), fc)], wi.at[c], w_sem.at[0, c]
        )

    def weight_out(c):
        return pltpu.make_async_copy(
            wout_ref.at[pl.ds(pl.multiple_of(c * fc, fc), fc), :], wo.at[c], w_sem.at[1, c]
        )

    def mine(k):
        src, dst = ((x_ref, xf), (g_ref, gf))[k]
        return pltpu.make_async_copy(src, dst.at[pl.ds(pl.multiple_of(col * rows, rows), rows), :], own_sem.at[k])

    for k in range(2):
        mine(k).start()

    def fetch(c, carry):
        weight_in(c).start()
        weight_out(c).start()
        return carry

    lax.fori_loop(0, nch, fetch, 0)

    barrier = pltpu.get_barrier_semaphore()
    for q in range(1, chips):
        pl.semaphore_signal(
            barrier, inc=1, device_id={"col": lax.rem(chip + q, chips) * 2 + core}, device_id_type=MESH
        )
    pl.semaphore_signal(barrier, inc=1, device_id={"col": chip * 2 + 1 - core}, device_id_type=MESH)
    pl.semaphore_signal(barrier, inc=1, device_id={"row": inner}, device_id_type=MESH)

    @pl.when(has_out)
    def _():
        pl.semaphore_signal(barrier, inc=1, device_id={"row": outer}, device_id_type=MESH)

    pl.semaphore_wait(barrier, chips + 1 + has_out.astype(jnp.int32))

    def block(k, owner):
        return (xf, gf)[k].at[pl.ds(pl.multiple_of(owner * rows, rows), rows), :]

    def far(k, q):
        return pltpu.make_async_remote_copy(
            src_ref=(x_ref, g_ref)[k],
            dst_ref=block(k, col),
            send_sem=ag_send.at[k, q],
            recv_sem=ag_recv.at[k, col],
            device_id={"col": lax.rem(chip + q, chips) * 2 + core},
            device_id_type=MESH,
        )

    def near(k, q):
        owner = lax.rem(chip + chips - q, chips) * 2 + core
        return pltpu.make_async_remote_copy(
            src_ref=x_ref if (q == 0 and k == 0) else g_ref if q == 0 else block(k, owner),
            dst_ref=block(k, owner),
            send_sem=ag_send.at[k, chips + q],
            recv_sem=ag_recv.at[k, owner],
            device_id={"col": chip * 2 + 1 - core},
            device_id_type=MESH,
        )

    def landed(k, owner):
        return pltpu.make_async_remote_copy(
            src_ref=block(k, owner),
            dst_ref=block(k, owner),
            send_sem=ag_send.at[k, 0],
            recv_sem=ag_recv.at[k, owner],
            device_id={"col": chip * 2 + 1 - core},
            device_id_type=MESH,
        )

    def pass_on(k):
        mine(k).wait()
        for q in range(1, chips):
            landed(k, lax.rem(chip + chips - q, chips) * 2 + core).wait_recv()
            near(k, q).start()

    def arrived(k):
        for q in range(chips):
            landed(k, lax.rem(chip + chips - q, chips) * 2 + 1 - core).wait_recv()
        pltpu.make_async_copy((xf, gf)[k], (x_out, g_out)[k], out_sem.at[k]).start()

    def begin(k):
        for q in range(1, chips):
            far(k, q).start()
        near(k, 0).start()

    begin(0)
    pass_on(0)
    begin(1)
    gi[...] = jnp.zeros_like(gi)
    arrived(0)

    def send_sum(c, k):
        return pltpu.make_async_remote_copy(
            src_ref=s.at[k, c], dst_ref=r.at[k, c], send_sem=s_send.at[k, c], recv_sem=s_recv.at[k, c],
            device_id={"row": inner}, device_id_type=MESH,
        )

    def swap_sum(c, k):
        return pltpu.make_async_remote_copy(
            src_ref=s.at[k, c, other], dst_ref=e.at[k, c], send_sem=e_send.at[k, c], recv_sem=e_recv.at[k, c],
            device_id={"row": inner}, device_id_type=MESH,
        )

    def send_hidden(c, half, target, way):
        return pltpu.make_async_remote_copy(
            src_ref=hb.at[c, half], dst_ref=hb.at[c, half],
            send_sem=h_send.at[c, half, way], recv_sem=h_recv.at[c, half],
            device_id={"row": target}, device_id_type=MESH,
        )

    def save_hidden(c):
        return pltpu.make_async_copy(hb.at[c], h_out.at[c], out_sem.at[3 + c])

    tokens = xf.shape[0]
    split = tokens // 2

    def local_sum(c, k):
        if k == 0:
            weight_in(c).wait()
            pf[0] = jnp.dot(xf[...], wi[c], preferred_element_type=f32).reshape(2, split, fc)
        else:
            weight_out(c).wait()
            pf[1] = nt_dot(gf[...], wo[c]).reshape(2, split, fc)

        @pl.when(has_out)
        def _():
            send_sum(c, k).wait_recv()
            pf[k] += r[k, c].astype(f32)

    def input_terms(c):
        save_hidden(c).start()
        grads = hb[c, :, 1].reshape(tokens, fc)
        gi[...] += nt_dot(grads, wi[c])

    @pl.when(jnp.logical_not(is_mid))
    def _():
        def inwards(k, c, carry):
            local_sum(c, k)
            s[k, c] = pf[k].astype(bf16)
            send_sum(c, k).start()
            return carry

        ahead = min(3, nch)
        lax.fori_loop(0, ahead, functools.partial(inwards, 0), 0)
        pass_on(1)
        arrived(1)
        lax.fori_loop(0, ahead, functools.partial(inwards, 1), 0)

        def inwards_both(c, carry):
            return inwards(1, c, inwards(0, c, carry))

        lax.fori_loop(ahead, nch, inwards_both, 0)

        def outwards(c, carry):
            for half in range(2):
                send_hidden(c, half, inner, 0).wait_recv()

                @pl.when(has_out)
                def _():
                    send_hidden(c, half, outer, 1).start()

            input_terms(c)
            return carry

        lax.fori_loop(0, nch, outwards, 0)

        def drain(c, carry):
            for k in range(2):
                send_sum(c, k).wait_send()

            @pl.when(has_out)
            def _():
                for half in range(2):
                    send_hidden(c, half, outer, 1).wait_send()

            return carry

        lax.fori_loop(0, nch, drain, 0)

    @pl.when(is_mid)
    def _():
        pass_on(1)
        arrived(1)

        def tick(t, carry):
            @pl.when(t < nch)
            def _():
                for k in range(2):
                    local_sum(t, k)
                    s[k, t, other] = pf[k, other].astype(bf16)
                    swap_sum(t, k).start()
                    keep[lax.rem(t, 2), k] = pf[k, side]

            @pl.when((t >= 1) & (t <= nch))
            def _():
                c = t - 1
                sums = []
                for k in range(2):
                    swap_sum(c, k).wait_recv()
                    sums.append(keep[lax.rem(c, 2), k] + e[k, c].astype(f32))
                hidden, hid_grad = gelu_pair(*sums)
                hb[c, side, 0] = hidden
                hb[c, side, 1] = hid_grad
                send_hidden(c, side, inner, 0).start()

                @pl.when(has_out)
                def _():
                    send_hidden(c, side, outer, 1).start()

            @pl.when(t >= 2)
            def _():
                c = t - 2
                send_hidden(c, other, inner, 0).wait_recv()

                @pl.when(has_out)
                def _():
                    send_hidden(c, other, outer, 1).start()

                input_terms(c)

            return carry

        lax.fori_loop(0, nch + 2, tick, 0)

        def drain(c, carry):
            for k in range(2):
                swap_sum(c, k).wait_send()
            send_hidden(c, side, inner, 0).wait_send()

            @pl.when(has_out)
            def _():
                send_hidden(c, side, outer, 1).wait_send()
                send_hidden(c, other, outer, 1).wait_send()

            return carry

        lax.fori_loop(0, nch, drain, 0)

    def own(chip_to, core_to):
        return pl.ds(pl.multiple_of((chip_to * 2 + core_to) * rows, rows), rows)

    def to_core(q):
        target = lax.rem(chip + q, chips)
        return pltpu.make_async_remote_copy(
            src_ref=gi.at[own(target, 1 - core), :], dst_ref=pair.at[q],
            send_sem=pair_send.at[q], recv_sem=pair_recv.at[q],
            device_id={"col": chip * 2 + 1 - core}, device_id_type=MESH,
        )

    def to_chip(q):
        return pltpu.make_async_remote_copy(
            src_ref=part.at[q], dst_ref=came.at[q],
            send_sem=part_send.at[q], recv_sem=part_recv.at[q],
            device_id={"col": lax.rem(chip + q, chips) * 2 + core}, device_id_type=MESH,
        )

    for q in range(chips - 1, -1, -1):
        to_core(q).start()
    for q in range(chips - 1, 0, -1):
        to_core(q).wait_recv()
        part[q] = (gi[own(lax.rem(chip + q, chips), core), :] + pair[q]).astype(bf16)
        to_chip(q).start()
    to_core(0).wait_recv()
    total = gi[own(chip, core), :] + pair[0]
    for q in range(chips - 1, 0, -1):
        to_chip(q).wait_recv()
        total = total + came[q].astype(f32)
    result[...] = total.astype(bf16)
    last = pltpu.make_async_copy(result, gi_out, out_sem.at[2])
    last.start()
    for q in range(chips):
        to_core(q).wait_send()
    for q in range(1, chips):
        to_chip(q).wait_send()
    for k in range(2):
        for q in range(1, chips):
            far(k, q).wait_send()
        for q in range(chips):
            near(k, q).wait_send()
    pltpu.make_async_copy(xf, x_out, out_sem.at[0]).wait()
    pltpu.make_async_copy(gf, g_out, out_sem.at[1]).wait()

    def saved(c, carry):
        save_hidden(c).wait()
        return carry

    lax.fori_loop(0, nch, saved, 0)
    last.wait()


def weights_kernel(nch, fc, x_ref, g_ref, hid_ref, all_ref, gwi_ref, gwo_ref):
    tokens = g_ref.shape[0]
    gwo_ref[...] = tn_dot(hid_ref[0, :, 0].reshape(tokens, fc), g_ref[...]).astype(bf16)
    turned = x_ref[...].T
    for c in range(nch):
        grads = all_ref[c, :, 1].reshape(tokens, fc)
        gwi_ref[:, c * fc : (c + 1) * fc] = jnp.dot(
            turned, grads, preferred_element_type=f32
        ).astype(bf16)


def on_device(n_row, n_col, inputs, out_grad, weight_in, weight_out):
    rows, d = inputs.shape
    f = weight_in.shape[1]
    tokens = rows * n_col
    fc = 256 if f % 256 == 0 else 128
    nch = f // fc
    split = tokens // 2
    any_spec = pl.BlockSpec(memory_space=pl.ANY)
    dma = pltpu.SemaphoreType.DMA
    hid, full_in, full_grad, grad_input = pl.pallas_call(
        functools.partial(exchange_kernel, n_row, n_col, nch, fc),
        out_shape=(
            jax.ShapeDtypeStruct((nch, 2, 2, split, fc), bf16),
            jax.ShapeDtypeStruct((tokens, d), bf16),
            jax.ShapeDtypeStruct((tokens, d), bf16),
            jax.ShapeDtypeStruct((rows, d), bf16),
        ),
        in_specs=[any_spec] * 4,
        out_specs=(any_spec,) * 4,
        scratch_shapes=[
            pltpu.VMEM((tokens, d), bf16),
            pltpu.VMEM((tokens, d), bf16),
            pltpu.VMEM((nch, d, fc), bf16),
            pltpu.VMEM((nch, fc, d), bf16),
            pltpu.VMEM((2, nch, 2, split, fc), bf16),
            pltpu.VMEM((2, nch, 2, split, fc), bf16),
            pltpu.VMEM((2, nch, split, fc), bf16),
            pltpu.VMEM((nch, 2, 2, split, fc), bf16),
            pltpu.VMEM((2, 2, split, fc), f32),
            pltpu.VMEM((2, 2, split, fc), f32),
            pltpu.VMEM((tokens, d), f32),
            pltpu.VMEM((n_col // 2, rows, d), f32),
            pltpu.VMEM((n_col // 2, rows, d), bf16),
            pltpu.VMEM((n_col // 2, rows, d), bf16),
            pltpu.VMEM((rows, d), bf16),
            dma((2, nch)),
            dma((2, n_col)),
            dma((2, n_col)),
            dma((2,)),
            dma((2, nch)),
            dma((2, nch)),
            dma((2, nch)),
            dma((2, nch)),
            dma((nch, 2, 2)),
            dma((nch, 2)),
            dma((3 + nch,)),
            dma((n_col // 2,)),
            dma((n_col // 2,)),
            dma((n_col // 2,)),
            dma((n_col // 2,)),
        ],
        compiler_params=pltpu.CompilerParams(
            collective_id=0, has_side_effects=True, vmem_limit_bytes=56 * 2**20
        ),
        cost_estimate=pl.CostEstimate(
            flops=6 * tokens * d * f, bytes_accessed=4 * d * f, transcendentals=tokens * f
        ),
        name="exchange",
    )(inputs, out_grad, weight_in, weight_out)

    wide = fc if d % nch else d // nch
    steps = nch
    grad_weight_in, grad_weight_out = pl.pallas_call(
        functools.partial(weights_kernel, nch, fc),
        grid=(steps,),
        out_shape=(jax.ShapeDtypeStruct((d, f), bf16), jax.ShapeDtypeStruct((f, d), bf16)),
        in_specs=[
            pl.BlockSpec((tokens, wide), lambda i: (0, i)),
            pl.BlockSpec((tokens, d), lambda i: (0, 0)),
            pl.BlockSpec((1, 2, 2, split, fc), lambda i: (i, 0, 0, 0, 0)),
            pl.BlockSpec((nch, 2, 2, split, fc), lambda i: (0, 0, 0, 0, 0)),
        ],
        out_specs=(
            pl.BlockSpec((wide, f), lambda i: (i, 0)),
            pl.BlockSpec((fc, d), lambda i: (i, 0)),
        ),
        compiler_params=pltpu.CompilerParams(vmem_limit_bytes=60 * 2**20),
        cost_estimate=pl.CostEstimate(
            flops=4 * tokens * d * f, bytes_accessed=4 * d * f, transcendentals=0
        ),
        name="weight_grads",
    )(full_in, full_grad, hid, hid)
    return (grad_input, grad_weight_in, grad_weight_out)


def solution(mesh):
    placed = (P("col", "row"), P("col", "row"), P("row", "col"), P("col", "row"))
    return jax.shard_map(
        functools.partial(on_device, mesh.shape["row"], mesh.shape["col"]),
        mesh=mesh,
        in_specs=placed,
        out_specs=(P("col", "row"), P("row", "col"), P("col", "row")),
        check_vma=False,
    )
```

```python
import functools

import jax
import jax.numpy as jnp
from jax import lax
from jax.experimental import pallas as pl
from jax.experimental.pallas import tpu as pltpu
from jax.sharding import PartitionSpec as P

gelu_cubic = 0.044715
root_two_pi = 0.7978845608028654
MESH = pl.DeviceIdType.MESH
bf16, f32 = jnp.bfloat16, jnp.float32


def gelu_pair(preact, act_grad):
    inner = root_two_pi * (preact + gelu_cubic * preact * preact * preact)
    tangent = jnp.tanh(inner)
    hidden = (0.5 * preact * (1.0 + tangent)).astype(bf16)
    slope = 0.5 * (1.0 + tangent) + 0.5 * preact * (1.0 - tangent * tangent) * root_two_pi * (
        1.0 + 3.0 * gelu_cubic * preact * preact
    )
    hid_grad = (act_grad * slope).astype(bf16)
    return (hidden, hid_grad)


def nt_dot(a, b):
    return lax.dot_general(a, b, (((1,), (1,)), ((), ())), preferred_element_type=f32)


def tn_dot(a, b):
    return lax.dot_general(a, b, (((0,), (0,)), ((), ())), preferred_element_type=f32)


def exchange_kernel(
    n_row, n_col, nch, fc,
    x_ref, g_ref, win_ref, wout_ref,
    *refs,
):
    h_out, x_out, g_out, own_out = refs[:4]
    part_out = refs[4 : 3 + n_col // 2]
    (
        xf, gf, wi, wo, s, r, e, hb, keep, pf, early, gi, pair, part,
        w_sem, ag_send, ag_recv, own_sem, s_send, s_recv, e_send, e_recv, h_send, h_recv, out_sem,
        pair_send, pair_recv, part_sem,
    ) = refs[3 + n_col // 2 :]
    row, col = lax.axis_index("row"), lax.axis_index("col")
    core, chip = lax.rem(col, 2), col // 2
    chips = n_col // 2
    rows = x_ref.shape[0]
    half_n = n_row // 2
    side = (row >= half_n).astype(jnp.int32)
    other = 1 - side
    place = jnp.where(side == 0, row, n_row - 1 - row)
    inner = jnp.where(side == 0, row + 1, row - 1)
    outer = jnp.where(side == 0, jnp.maximum(row - 1, 0), jnp.minimum(row + 1, n_row - 1))
    has_out = place > 0
    is_mid = place == half_n - 1

    def weight_in(c):
        return pltpu.make_async_copy(
            win_ref.at[:, pl.ds(pl.multiple_of(c * fc, fc), fc)], wi.at[c], w_sem.at[0, c]
        )

    def weight_out(c):
        return pltpu.make_async_copy(
            wout_ref.at[pl.ds(pl.multiple_of(c * fc, fc), fc), :], wo.at[c], w_sem.at[1, c]
        )

    def mine(k):
        src, dst = ((x_ref, xf), (g_ref, gf))[k]
        return pltpu.make_async_copy(src, dst.at[pl.ds(pl.multiple_of(col * rows, rows), rows), :], own_sem.at[k])

    for k in range(2):
        mine(k).start()

    def fetch(c, carry):
        weight_in(c).start()
        weight_out(c).start()
        return carry

    lax.fori_loop(0, nch, fetch, 0)

    barrier = pltpu.get_barrier_semaphore()
    for q in range(1, chips):
        pl.semaphore_signal(
            barrier, inc=1, device_id={"col": lax.rem(chip + q, chips) * 2 + core}, device_id_type=MESH
        )
    pl.semaphore_signal(barrier, inc=1, device_id={"col": chip * 2 + 1 - core}, device_id_type=MESH)
    pl.semaphore_signal(barrier, inc=1, device_id={"row": inner}, device_id_type=MESH)

    @pl.when(has_out)
    def _():
        pl.semaphore_signal(barrier, inc=1, device_id={"row": outer}, device_id_type=MESH)

    pl.semaphore_wait(barrier, chips + 1 + has_out.astype(jnp.int32))

    def block(k, owner):
        return (xf, gf)[k].at[pl.ds(pl.multiple_of(owner * rows, rows), rows), :]

    def far(k, q):
        return pltpu.make_async_remote_copy(
            src_ref=(x_ref, g_ref)[k],
            dst_ref=block(k, col),
            send_sem=ag_send.at[k, q],
            recv_sem=ag_recv.at[k, col],
            device_id={"col": lax.rem(chip + q, chips) * 2 + core},
            device_id_type=MESH,
        )

    def near(k, q):
        owner = lax.rem(chip + chips - q, chips) * 2 + core
        return pltpu.make_async_remote_copy(
            src_ref=x_ref if (q == 0 and k == 0) else g_ref if q == 0 else block(k, owner),
            dst_ref=block(k, owner),
            send_sem=ag_send.at[k, chips + q],
            recv_sem=ag_recv.at[k, owner],
            device_id={"col": chip * 2 + 1 - core},
            device_id_type=MESH,
        )

    def landed(k, owner):
        return pltpu.make_async_remote_copy(
            src_ref=block(k, owner),
            dst_ref=block(k, owner),
            send_sem=ag_send.at[k, 0],
            recv_sem=ag_recv.at[k, owner],
            device_id={"col": chip * 2 + 1 - core},
            device_id_type=MESH,
        )

    def pass_on(k):
        mine(k).wait()
        for q in range(1, chips):
            landed(k, lax.rem(chip + chips - q, chips) * 2 + core).wait_recv()
            near(k, q).start()

    def arrived(k):
        for q in range(chips):
            landed(k, lax.rem(chip + chips - q, chips) * 2 + 1 - core).wait_recv()
        pltpu.make_async_copy((xf, gf)[k], (x_out, g_out)[k], out_sem.at[k]).start()

    def begin(k):
        for q in range(1, chips):
            far(k, q).start()
        near(k, 0).start()

    begin(0)
    pass_on(0)
    begin(1)
    gi[...] = jnp.zeros_like(gi)
    arrived(0)

    def send_sum(c, k):
        return pltpu.make_async_remote_copy(
            src_ref=s.at[k, c], dst_ref=r.at[k, c], send_sem=s_send.at[k, c], recv_sem=s_recv.at[k, c],
            device_id={"row": inner}, device_id_type=MESH,
        )

    def swap_sum(c, k):
        return pltpu.make_async_remote_copy(
            src_ref=s.at[k, c, other], dst_ref=e.at[k, c], send_sem=e_send.at[k, c], recv_sem=e_recv.at[k, c],
            device_id={"row": inner}, device_id_type=MESH,
        )

    def send_hidden(c, half, target, way):
        return pltpu.make_async_remote_copy(
            src_ref=hb.at[c, half], dst_ref=hb.at[c, half],
            send_sem=h_send.at[c, half, way], recv_sem=h_recv.at[c, half],
            device_id={"row": target}, device_id_type=MESH,
        )

    def save_hidden(c):
        return pltpu.make_async_copy(hb.at[c], h_out.at[c], out_sem.at[3 + c])

    tokens = xf.shape[0]
    split = tokens // 2

    def pre_terms(c):
        weight_in(c).wait()
        return jnp.dot(xf[...], wi[c], preferred_element_type=f32).reshape(2, split, fc)

    ahead = early.shape[0]

    def work_ahead(c, carry):
        early[c] = pre_terms(c)
        return carry

    def local_sum(c, k):
        if k == 0:
            @pl.when(c < ahead)
            def _():
                pf[0] = early[jnp.minimum(c, ahead - 1)]

            @pl.when(c >= ahead)
            def _():
                pf[0] = pre_terms(c)

        else:
            weight_out(c).wait()
            pf[1] = nt_dot(gf[...], wo[c]).reshape(2, split, fc)

        @pl.when(has_out)
        def _():
            send_sum(c, k).wait_recv()
            pf[k] += r[k, c].astype(f32)

    def input_terms(c):
        save_hidden(c).start()
        grads = hb[c, :, 1].reshape(tokens, fc)
        for at in range(0, gi.shape[1], fc):
            gi[:, at : at + fc] += nt_dot(grads, wi[c, at : at + fc, :])

    @pl.when(jnp.logical_not(is_mid))
    def _():
        def inwards(k, c, carry):
            local_sum(c, k)
            s[k, c] = pf[k].astype(bf16)
            send_sum(c, k).start()
            return carry

        def inwards_ahead(c, carry):
            work_ahead(c, carry)
            return inwards(0, c, carry)

        lax.fori_loop(0, ahead, inwards_ahead, 0)
        pass_on(1)
        arrived(1)
        lax.fori_loop(0, ahead, functools.partial(inwards, 1), 0)

        def inwards_both(c, carry):
            return inwards(1, c, inwards(0, c, carry))

        lax.fori_loop(ahead, nch, inwards_both, 0)

        def outwards(c, carry):
            for half in range(2):
                send_hidden(c, half, inner, 0).wait_recv()

                @pl.when(has_out)
                def _():
                    send_hidden(c, half, outer, 1).start()

            input_terms(c)
            return carry

        lax.fori_loop(0, nch, outwards, 0)

        def drain(c, carry):
            for k in range(2):
                send_sum(c, k).wait_send()

            @pl.when(has_out)
            def _():
                for half in range(2):
                    send_hidden(c, half, outer, 1).wait_send()

            return carry

        lax.fori_loop(0, nch, drain, 0)

    @pl.when(is_mid)
    def _():
        lax.fori_loop(0, ahead, work_ahead, 0)
        pass_on(1)
        arrived(1)

        def tick(t, carry):
            @pl.when(t < nch)
            def _():
                for k in range(2):
                    local_sum(t, k)
                    s[k, t, other] = pf[k, other].astype(bf16)
                    swap_sum(t, k).start()
                    keep[lax.rem(t, 2), k] = pf[k, side]

            @pl.when((t >= 1) & (t <= nch))
            def _():
                c = t - 1
                sums = []
                for k in range(2):
                    swap_sum(c, k).wait_recv()
                    sums.append(keep[lax.rem(c, 2), k] + e[k, c].astype(f32))
                hidden, hid_grad = gelu_pair(*sums)
                hb[c, side, 0] = hidden
                hb[c, side, 1] = hid_grad
                send_hidden(c, side, inner, 0).start()

                @pl.when(has_out)
                def _():
                    send_hidden(c, side, outer, 1).start()

            @pl.when(t >= 2)
            def _():
                c = t - 2
                send_hidden(c, other, inner, 0).wait_recv()

                @pl.when(has_out)
                def _():
                    send_hidden(c, other, outer, 1).start()

                input_terms(c)

            return carry

        lax.fori_loop(0, nch + 2, tick, 0)

        def drain(c, carry):
            for k in range(2):
                swap_sum(c, k).wait_send()
            send_hidden(c, side, inner, 0).wait_send()

            @pl.when(has_out)
            def _():
                send_hidden(c, side, outer, 1).wait_send()
                send_hidden(c, other, outer, 1).wait_send()

            return carry

        lax.fori_loop(0, nch, drain, 0)

    def own(chip_to, core_to):
        return pl.ds(pl.multiple_of((chip_to * 2 + core_to) * rows, rows), rows)

    def to_core(q):
        target = lax.rem(chip + q, chips)
        return pltpu.make_async_remote_copy(
            src_ref=gi.at[own(target, 1 - core), :], dst_ref=pair.at[q],
            send_sem=pair_send.at[q], recv_sem=pair_recv.at[q],
            device_id={"col": chip * 2 + 1 - core}, device_id_type=MESH,
        )

    def hand_out(q):
        if q == 0:
            return pltpu.make_async_copy(pair.at[0], own_out, part_sem.at[0])
        return pltpu.make_async_copy(part.at[q], part_out[q - 1], part_sem.at[q])

    for q in range(chips - 1, -1, -1):
        to_core(q).start()
    for q in range(chips - 1, -1, -1):
        to_core(q).wait_recv()
        both = gi[own(lax.rem(chip + q, chips), core), :] + pair[q]
        if q == 0:
            pair[0] = both
        else:
            part[q] = both.astype(bf16)
        hand_out(q).start()
    for q in range(chips):
        to_core(q).wait_send()
        hand_out(q).wait()
    for k in range(2):
        for q in range(1, chips):
            far(k, q).wait_send()
        for q in range(chips):
            near(k, q).wait_send()
    pltpu.make_async_copy(xf, x_out, out_sem.at[0]).wait()
    pltpu.make_async_copy(gf, g_out, out_sem.at[1]).wait()

    def saved(c, carry):
        save_hidden(c).wait()
        return carry

    lax.fori_loop(0, nch, saved, 0)


def weights_kernel(nch, fc, x_ref, g_ref, hid_ref, all_ref, gwi_ref, gwo_ref):
    tokens = g_ref.shape[0]
    turned = hid_ref[0, :, 0].reshape(tokens, fc).T
    for at in range(0, g_ref.shape[1], fc):
        gwo_ref[:, at : at + fc] = jnp.dot(
            turned, g_ref[:, at : at + fc], preferred_element_type=f32
        ).astype(bf16)
    turned = x_ref[...].T
    for c in range(nch):
        grads = all_ref[c, :, 1].reshape(tokens, fc)
        gwi_ref[:, c * fc : (c + 1) * fc] = jnp.dot(
            turned, grads, preferred_element_type=f32
        ).astype(bf16)


def on_device(n_row, n_col, inputs, out_grad, weight_in, weight_out):
    rows, d = inputs.shape
    f = weight_in.shape[1]
    tokens = rows * n_col
    fc = 256 if f % 256 == 0 else 128
    nch = f // fc
    split = tokens // 2
    chips = n_col // 2
    any_spec = pl.BlockSpec(memory_space=pl.ANY)
    dma = pltpu.SemaphoreType.DMA
    hid, full_in, full_grad, own, *parts = pl.pallas_call(
        functools.partial(exchange_kernel, n_row, n_col, nch, fc),
        out_shape=(
            jax.ShapeDtypeStruct((nch, 2, 2, split, fc), bf16),
            jax.ShapeDtypeStruct((tokens, d), bf16),
            jax.ShapeDtypeStruct((tokens, d), bf16),
            jax.ShapeDtypeStruct((rows, d), f32),
        )
        + (jax.ShapeDtypeStruct((rows, d), bf16),) * (chips - 1),
        in_specs=[any_spec] * 4,
        out_specs=(any_spec,) * (3 + chips),
        scratch_shapes=[
            pltpu.VMEM((tokens, d), bf16),
            pltpu.VMEM((tokens, d), bf16),
            pltpu.VMEM((nch, d, fc), bf16),
            pltpu.VMEM((nch, fc, d), bf16),
            pltpu.VMEM((2, nch, 2, split, fc), bf16),
            pltpu.VMEM((2, nch, 2, split, fc), bf16),
            pltpu.VMEM((2, nch, split, fc), bf16),
            pltpu.VMEM((nch, 2, 2, split, fc), bf16),
            pltpu.VMEM((2, 2, split, fc), f32),
            pltpu.VMEM((2, 2, split, fc), f32),
            pltpu.VMEM((min(4, nch), 2, split, fc), f32),
            pltpu.VMEM((tokens, d), f32),
            pltpu.VMEM((chips, rows, d), f32),
            pltpu.VMEM((chips, rows, d), bf16),
            dma((2, nch)),
            dma((2, n_col)),
            dma((2, n_col)),
            dma((2,)),
            dma((2, nch)),
            dma((2, nch)),
            dma((2, nch)),
            dma((2, nch)),
            dma((nch, 2, 2)),
            dma((nch, 2)),
            dma((3 + nch,)),
            dma((chips,)),
            dma((chips,)),
            dma((chips,)),
        ],
        compiler_params=pltpu.CompilerParams(
            collective_id=0, has_side_effects=True, vmem_limit_bytes=56 * 2**20
        ),
        cost_estimate=pl.CostEstimate(
            flops=6 * tokens * d * f, bytes_accessed=4 * d * f, transcendentals=tokens * f
        ),
        name="exchange",
    )(inputs, out_grad, weight_in, weight_out)

    moved = [
        lax.ppermute(
            term, "col", [(c, ((c // 2 + q) % chips) * 2 + c % 2) for c in range(n_col)]
        )
        for q, term in enumerate(parts, 1)
    ]
    wide = fc if d % nch else d // nch
    steps = nch
    grad_weight_in, grad_weight_out = pl.pallas_call(
        functools.partial(weights_kernel, nch, fc),
        grid=(steps,),
        out_shape=(jax.ShapeDtypeStruct((d, f), bf16), jax.ShapeDtypeStruct((f, d), bf16)),
        in_specs=[
            pl.BlockSpec((tokens, wide), lambda i: (0, i)),
            pl.BlockSpec((tokens, d), lambda i: (0, 0)),
            pl.BlockSpec((1, 2, 2, split, fc), lambda i: (i, 0, 0, 0, 0)),
            pl.BlockSpec((nch, 2, 2, split, fc), lambda i: (0, 0, 0, 0, 0)),
        ],
        out_specs=(
            pl.BlockSpec((wide, f), lambda i: (i, 0)),
            pl.BlockSpec((fc, d), lambda i: (i, 0)),
        ),
        compiler_params=pltpu.CompilerParams(vmem_limit_bytes=60 * 2**20),
        cost_estimate=pl.CostEstimate(
            flops=4 * tokens * d * f, bytes_accessed=4 * d * f, transcendentals=0
        ),
        name="weight_grads",
    )(full_in, full_grad, hid, hid)
    total = own
    for term in moved:
        total = total + term.astype(f32)
    return (total.astype(bf16), grad_weight_in, grad_weight_out)


def solution(mesh):
    placed = (P("col", "row"), P("col", "row"), P("row", "col"), P("col", "row"))
    return jax.shard_map(
        functools.partial(on_device, mesh.shape["row"], mesh.shape["col"]),
        mesh=mesh,
        in_specs=placed,
        out_specs=(P("col", "row"), P("row", "col"), P("col", "row")),
        check_vma=False,
    )
```

```python
import functools

import jax
import jax.numpy as jnp
from jax import lax
from jax.experimental import pallas as pl
from jax.experimental.pallas import tpu as pltpu
from jax.sharding import PartitionSpec as P

gelu_cubic = 0.044715
root_two_pi = 0.7978845608028654
MESH = pl.DeviceIdType.MESH
tall = 1024
bf16, f32 = jnp.bfloat16, jnp.float32


def gelu_pair(preact, act_grad):
    inner = root_two_pi * (preact + gelu_cubic * preact * preact * preact)
    tangent = jnp.tanh(inner)
    hidden = (0.5 * preact * (1.0 + tangent)).astype(bf16)
    slope = 0.5 * (1.0 + tangent) + 0.5 * preact * (1.0 - tangent * tangent) * root_two_pi * (
        1.0 + 3.0 * gelu_cubic * preact * preact
    )
    hid_grad = (act_grad * slope).astype(bf16)
    return (hidden, hid_grad)


def nt_dot(a, b):
    return lax.dot_general(a, b, (((1,), (1,)), ((), ())), preferred_element_type=f32)


def exchange_kernel(
    n_row, n_col, nch, fc,
    x_ref, g_ref, win_ref, wout_ref,
    *refs,
):
    h_out, x_out, g_out, own_out = refs[:4]
    part_out = refs[4 : 3 + n_col // 2]
    (
        xf, gf, wi, wo, s, r, e, hb, keep, pf, early, gi, turned, pair, part,
        w_sem, ag_send, ag_recv, own_sem, s_send, s_recv, e_send, e_recv, h_send, h_recv, out_sem,
        pair_send, pair_recv, part_sem,
    ) = refs[3 + n_col // 2 :]
    row, col = lax.axis_index("row"), lax.axis_index("col")
    core, chip = lax.rem(col, 2), col // 2
    chips = n_col // 2
    rows = x_ref.shape[0]
    half_n = n_row // 2
    side = (row >= half_n).astype(jnp.int32)
    other = 1 - side
    place = jnp.where(side == 0, row, n_row - 1 - row)
    inner = jnp.where(side == 0, row + 1, row - 1)
    outer = jnp.where(side == 0, jnp.maximum(row - 1, 0), jnp.minimum(row + 1, n_row - 1))
    has_out = place > 0
    is_mid = place == half_n - 1

    def weight_in(c):
        return pltpu.make_async_copy(
            win_ref.at[:, pl.ds(pl.multiple_of(c * fc, fc), fc)], wi.at[c], w_sem.at[0, c]
        )

    def weight_out(c):
        return pltpu.make_async_copy(
            wout_ref.at[pl.ds(pl.multiple_of(c * fc, fc), fc), :], wo.at[c], w_sem.at[1, c]
        )

    def mine(k):
        src, dst = ((x_ref, xf), (g_ref, gf))[k]
        return pltpu.make_async_copy(src, dst.at[pl.ds(pl.multiple_of(col * rows, rows), rows), :], own_sem.at[k])

    for k in range(2):
        mine(k).start()

    def fetch(c, carry):
        weight_in(c).start()
        weight_out(c).start()
        return carry

    lax.fori_loop(0, nch, fetch, 0)

    barrier = pltpu.get_barrier_semaphore()
    for q in range(1, chips):
        pl.semaphore_signal(
            barrier, inc=1, device_id={"col": lax.rem(chip + q, chips) * 2 + core}, device_id_type=MESH
        )
    pl.semaphore_signal(barrier, inc=1, device_id={"col": chip * 2 + 1 - core}, device_id_type=MESH)
    pl.semaphore_signal(barrier, inc=1, device_id={"row": inner}, device_id_type=MESH)

    @pl.when(has_out)
    def _():
        pl.semaphore_signal(barrier, inc=1, device_id={"row": outer}, device_id_type=MESH)

    pl.semaphore_wait(barrier, chips + 1 + has_out.astype(jnp.int32))

    def block(k, owner):
        return (xf, gf)[k].at[pl.ds(pl.multiple_of(owner * rows, rows), rows), :]

    def far(k, q):
        return pltpu.make_async_remote_copy(
            src_ref=(x_ref, g_ref)[k],
            dst_ref=block(k, col),
            send_sem=ag_send.at[k, q],
            recv_sem=ag_recv.at[k, col],
            device_id={"col": lax.rem(chip + q, chips) * 2 + core},
            device_id_type=MESH,
        )

    def near(k, q):
        owner = lax.rem(chip + chips - q, chips) * 2 + core
        return pltpu.make_async_remote_copy(
            src_ref=x_ref if (q == 0 and k == 0) else g_ref if q == 0 else block(k, owner),
            dst_ref=block(k, owner),
            send_sem=ag_send.at[k, chips + q],
            recv_sem=ag_recv.at[k, owner],
            device_id={"col": chip * 2 + 1 - core},
            device_id_type=MESH,
        )

    def landed(k, owner):
        return pltpu.make_async_remote_copy(
            src_ref=block(k, owner),
            dst_ref=block(k, owner),
            send_sem=ag_send.at[k, 0],
            recv_sem=ag_recv.at[k, owner],
            device_id={"col": chip * 2 + 1 - core},
            device_id_type=MESH,
        )

    def pass_on(k):
        mine(k).wait()
        for q in range(1, chips):
            landed(k, lax.rem(chip + chips - q, chips) * 2 + core).wait_recv()
            near(k, q).start()

    def arrived(k):
        for q in range(chips):
            landed(k, lax.rem(chip + chips - q, chips) * 2 + 1 - core).wait_recv()
        pltpu.make_async_copy((xf, gf)[k], (x_out, g_out)[k], out_sem.at[k]).start()

    def begin(k):
        for q in range(1, chips):
            far(k, q).start()
        near(k, 0).start()

    begin(0)
    pass_on(0)
    begin(1)
    turned[...] = jnp.zeros_like(turned)
    arrived(0)

    def send_sum(c, k):
        return pltpu.make_async_remote_copy(
            src_ref=s.at[k, c], dst_ref=r.at[k, c], send_sem=s_send.at[k, c], recv_sem=s_recv.at[k, c],
            device_id={"row": inner}, device_id_type=MESH,
        )

    def swap_sum(c, k):
        return pltpu.make_async_remote_copy(
            src_ref=s.at[k, c, other], dst_ref=e.at[k, c], send_sem=e_send.at[k, c], recv_sem=e_recv.at[k, c],
            device_id={"row": inner}, device_id_type=MESH,
        )

    def send_hidden(c, half, target, way):
        return pltpu.make_async_remote_copy(
            src_ref=hb.at[c, half], dst_ref=hb.at[c, half],
            send_sem=h_send.at[c, half, way], recv_sem=h_recv.at[c, half],
            device_id={"row": target}, device_id_type=MESH,
        )

    def save_hidden(c):
        return pltpu.make_async_copy(hb.at[c], h_out.at[c], out_sem.at[3 + c])

    tokens = xf.shape[0]
    split = tokens // 2

    def pre_terms(c):
        weight_in(c).wait()
        return jnp.dot(xf[...], wi[c], preferred_element_type=f32).reshape(2, split, fc)

    ahead = early.shape[0]

    def work_ahead(c, carry):
        early[c] = pre_terms(c)
        return carry

    def local_sum(c, k):
        if k == 0:
            @pl.when(c < ahead)
            def _():
                pf[0] = early[jnp.minimum(c, ahead - 1)]

            @pl.when(c >= ahead)
            def _():
                pf[0] = pre_terms(c)

        else:
            weight_out(c).wait()
            pf[1] = nt_dot(gf[...], wo[c]).reshape(2, split, fc)

        @pl.when(has_out)
        def _():
            send_sum(c, k).wait_recv()
            pf[k] += r[k, c].astype(f32)

    def input_terms(c):
        save_hidden(c).start()
        grads = hb[c, :, 1].reshape(tokens, fc).T
        for at in range(0, turned.shape[0], tall):
            end = min(at + tall, turned.shape[0])
            turned[at:end, :] += jnp.dot(wi[c, at:end, :], grads, preferred_element_type=f32)

    @pl.when(jnp.logical_not(is_mid))
    def _():
        def inwards(k, c, carry):
            local_sum(c, k)
            s[k, c] = pf[k].astype(bf16)
            send_sum(c, k).start()
            return carry

        def inwards_ahead(c, carry):
            work_ahead(c, carry)
            return inwards(0, c, carry)

        lax.fori_loop(0, ahead, inwards_ahead, 0)
        pass_on(1)
        arrived(1)
        lax.fori_loop(0, ahead, functools.partial(inwards, 1), 0)

        def inwards_both(c, carry):
            return inwards(1, c, inwards(0, c, carry))

        lax.fori_loop(ahead, nch, inwards_both, 0)

        def outwards(c, carry):
            for half in range(2):
                send_hidden(c, half, inner, 0).wait_recv()

                @pl.when(has_out)
                def _():
                    send_hidden(c, half, outer, 1).start()

            input_terms(c)
            return carry

        lax.fori_loop(0, nch, outwards, 0)

        def drain(c, carry):
            for k in range(2):
                send_sum(c, k).wait_send()

            @pl.when(has_out)
            def _():
                for half in range(2):
                    send_hidden(c, half, outer, 1).wait_send()

            return carry

        lax.fori_loop(0, nch, drain, 0)

    @pl.when(is_mid)
    def _():
        lax.fori_loop(0, ahead, work_ahead, 0)
        pass_on(1)
        arrived(1)

        def tick(t, carry):
            @pl.when(t < nch)
            def _():
                for k in range(2):
                    local_sum(t, k)
                    s[k, t, other] = pf[k, other].astype(bf16)
                    swap_sum(t, k).start()
                    keep[lax.rem(t, 2), k] = pf[k, side]

            @pl.when((t >= 1) & (t <= nch))
            def _():
                c = t - 1
                sums = []
                for k in range(2):
                    swap_sum(c, k).wait_recv()
                    sums.append(keep[lax.rem(c, 2), k] + e[k, c].astype(f32))
                hidden, hid_grad = gelu_pair(*sums)
                hb[c, side, 0] = hidden
                hb[c, side, 1] = hid_grad
                send_hidden(c, side, inner, 0).start()

                @pl.when(has_out)
                def _():
                    send_hidden(c, side, outer, 1).start()

            @pl.when(t >= 2)
            def _():
                c = t - 2
                send_hidden(c, other, inner, 0).wait_recv()

                @pl.when(has_out)
                def _():
                    send_hidden(c, other, outer, 1).start()

                input_terms(c)

            return carry

        lax.fori_loop(0, nch + 2, tick, 0)

        def drain(c, carry):
            for k in range(2):
                swap_sum(c, k).wait_send()
            send_hidden(c, side, inner, 0).wait_send()

            @pl.when(has_out)
            def _():
                send_hidden(c, side, outer, 1).wait_send()
                send_hidden(c, other, outer, 1).wait_send()

            return carry

        lax.fori_loop(0, nch, drain, 0)

    def own(chip_to, core_to):
        return pl.ds(pl.multiple_of((chip_to * 2 + core_to) * rows, rows), rows)

    def to_core(q):
        target = lax.rem(chip + q, chips)
        return pltpu.make_async_remote_copy(
            src_ref=gi.at[own(target, 1 - core), :], dst_ref=pair.at[q],
            send_sem=pair_send.at[q], recv_sem=pair_recv.at[q],
            device_id={"col": chip * 2 + 1 - core}, device_id_type=MESH,
        )

    def hand_out(q):
        if q == 0:
            return pltpu.make_async_copy(pair.at[0], own_out, part_sem.at[0])
        return pltpu.make_async_copy(part.at[q], part_out[q - 1], part_sem.at[q])

    for at in range(0, turned.shape[0], fc):
        gi[:, at : at + fc] = turned[at : at + fc, :].T
    for q in range(chips - 1, -1, -1):
        to_core(q).start()
    for q in range(chips - 1, -1, -1):
        to_core(q).wait_recv()
        both = gi[own(lax.rem(chip + q, chips), core), :] + pair[q]
        if q == 0:
            pair[0] = both
        else:
            part[q] = both.astype(bf16)
        hand_out(q).start()
    for q in range(chips):
        to_core(q).wait_send()
        hand_out(q).wait()
    for k in range(2):
        for q in range(1, chips):
            far(k, q).wait_send()
        for q in range(chips):
            near(k, q).wait_send()
    pltpu.make_async_copy(xf, x_out, out_sem.at[0]).wait()
    pltpu.make_async_copy(gf, g_out, out_sem.at[1]).wait()

    def saved(c, carry):
        save_hidden(c).wait()
        return carry

    lax.fori_loop(0, nch, saved, 0)


def weights_kernel(nch, fc, x_ref, g_ref, hid_ref, all_ref, gwi_ref, gwo_ref, xt, ht):
    tokens = x_ref.shape[0]

    @pl.when(pl.program_id(0) == 0)
    def _():
        xt[...] = x_ref[...].T
        for c in range(nch):
            ht[c * fc : (c + 1) * fc, :] = all_ref[c, :, 0].reshape(tokens, fc).T

    grads = hid_ref[0, :, 1].reshape(tokens, fc)
    for out, left, right in ((gwi_ref, xt, grads), (gwo_ref, ht, g_ref[...])):
        for at in range(0, left.shape[0], tall):
            end = min(at + tall, left.shape[0])
            out[at:end, :] = jnp.dot(left[at:end, :], right, preferred_element_type=f32).astype(bf16)


def on_device(n_row, n_col, inputs, out_grad, weight_in, weight_out):
    rows, d = inputs.shape
    f = weight_in.shape[1]
    tokens = rows * n_col
    fc = 256 if f % 256 == 0 else 128
    nch = f // fc
    split = tokens // 2
    chips = n_col // 2
    any_spec = pl.BlockSpec(memory_space=pl.ANY)
    dma = pltpu.SemaphoreType.DMA
    hid, full_in, full_grad, own, *parts = pl.pallas_call(
        functools.partial(exchange_kernel, n_row, n_col, nch, fc),
        out_shape=(
            jax.ShapeDtypeStruct((nch, 2, 2, split, fc), bf16),
            jax.ShapeDtypeStruct((tokens, d), bf16),
            jax.ShapeDtypeStruct((tokens, d), bf16),
            jax.ShapeDtypeStruct((rows, d), f32),
        )
        + (jax.ShapeDtypeStruct((rows, d), bf16),) * (chips - 1),
        in_specs=[any_spec] * 4,
        out_specs=(any_spec,) * (3 + chips),
        scratch_shapes=[
            pltpu.VMEM((tokens, d), bf16),
            pltpu.VMEM((tokens, d), bf16),
            pltpu.VMEM((nch, d, fc), bf16),
            pltpu.VMEM((nch, fc, d), bf16),
            pltpu.VMEM((2, nch, 2, split, fc), bf16),
            pltpu.VMEM((2, nch, 2, split, fc), bf16),
            pltpu.VMEM((2, nch, split, fc), bf16),
            pltpu.VMEM((nch, 2, 2, split, fc), bf16),
            pltpu.VMEM((2, 2, split, fc), f32),
            pltpu.VMEM((2, 2, split, fc), f32),
            pltpu.VMEM((min(4, nch), 2, split, fc), f32),
            pltpu.VMEM((tokens, d), f32),
            pltpu.VMEM((d, tokens), f32),
            pltpu.VMEM((chips, rows, d), f32),
            pltpu.VMEM((chips, rows, d), bf16),
            dma((2, nch)),
            dma((2, n_col)),
            dma((2, n_col)),
            dma((2,)),
            dma((2, nch)),
            dma((2, nch)),
            dma((2, nch)),
            dma((2, nch)),
            dma((nch, 2, 2)),
            dma((nch, 2)),
            dma((3 + nch,)),
            dma((chips,)),
            dma((chips,)),
            dma((chips,)),
        ],
        compiler_params=pltpu.CompilerParams(
            collective_id=0, has_side_effects=True, vmem_limit_bytes=56 * 2**20
        ),
        cost_estimate=pl.CostEstimate(
            flops=6 * tokens * d * f, bytes_accessed=4 * d * f, transcendentals=tokens * f
        ),
        name="exchange",
    )(inputs, out_grad, weight_in, weight_out)

    moved = [
        lax.ppermute(
            term, "col", [(c, ((c // 2 + q) % chips) * 2 + c % 2) for c in range(n_col)]
        )
        for q, term in enumerate(parts, 1)
    ]
    wide = d // nch
    grad_weight_in, grad_weight_out = pl.pallas_call(
        functools.partial(weights_kernel, nch, fc),
        grid=(nch,),
        out_shape=(jax.ShapeDtypeStruct((d, f), bf16), jax.ShapeDtypeStruct((f, d), bf16)),
        in_specs=[
            pl.BlockSpec((tokens, d), lambda i: (0, 0)),
            pl.BlockSpec((tokens, wide), lambda i: (0, i)),
            pl.BlockSpec((1, 2, 2, split, fc), lambda i: (i, 0, 0, 0, 0)),
            pl.BlockSpec((nch, 2, 2, split, fc), lambda i: (0, 0, 0, 0, 0)),
        ],
        out_specs=(
            pl.BlockSpec((d, fc), lambda i: (0, i)),
            pl.BlockSpec((f, wide), lambda i: (0, i)),
        ),
        scratch_shapes=[pltpu.VMEM((d, tokens), bf16), pltpu.VMEM((f, tokens), bf16)],
        compiler_params=pltpu.CompilerParams(vmem_limit_bytes=60 * 2**20),
        cost_estimate=pl.CostEstimate(
            flops=4 * tokens * d * f, bytes_accessed=4 * d * f, transcendentals=0
        ),
        name="weight_grads",
    )(full_in, full_grad, hid, hid)
    total = own
    for term in moved:
        total = total + term.astype(f32)
    return (total.astype(bf16), grad_weight_in, grad_weight_out)


def solution(mesh):
    placed = (P("col", "row"), P("col", "row"), P("row", "col"), P("col", "row"))
    return jax.shard_map(
        functools.partial(on_device, mesh.shape["row"], mesh.shape["col"]),
        mesh=mesh,
        in_specs=placed,
        out_specs=(P("col", "row"), P("row", "col"), P("col", "row")),
        check_vma=False,
    )
```

```python
import functools

import jax
import jax.numpy as jnp
from jax import lax
from jax.experimental import pallas as pl
from jax.experimental.pallas import tpu as pltpu
from jax.sharding import PartitionSpec as P

gelu_cubic = 0.044715
root_two_pi = 0.7978845608028654
MESH = pl.DeviceIdType.MESH
bf16, f32 = jnp.bfloat16, jnp.float32


def gelu_pair(preact, act_grad):
    inner = root_two_pi * (preact + gelu_cubic * preact * preact * preact)
    tangent = jnp.tanh(inner)
    hidden = (0.5 * preact * (1.0 + tangent)).astype(bf16)
    slope = 0.5 * (1.0 + tangent) + 0.5 * preact * (1.0 - tangent * tangent) * root_two_pi * (
        1.0 + 3.0 * gelu_cubic * preact * preact
    )
    hid_grad = (act_grad * slope).astype(bf16)
    return (hidden, hid_grad)


def nt_dot(a, b):
    return lax.dot_general(a, b, (((1,), (1,)), ((), ())), preferred_element_type=f32)


def tn_dot(a, b):
    return lax.dot_general(a, b, (((0,), (0,)), ((), ())), preferred_element_type=f32)


def exchange_kernel(
    n_row, n_col, nch, fc,
    x_ref, g_ref, win_ref, wout_ref,
    *refs,
):
    h_out, x_out, g_out, own_out = refs[:4]
    part_out = refs[4 : 3 + n_col // 2]
    (
        xf, gf, wi, wo, s, r, e, hb, keep, pf, early, gi, pair, part,
        w_sem, ag_send, ag_recv, own_sem, s_send, s_recv, e_send, e_recv, h_send, h_recv, out_sem,
        pair_send, pair_recv, part_sem,
    ) = refs[3 + n_col // 2 :]
    row, col = lax.axis_index("row"), lax.axis_index("col")
    core, chip = lax.rem(col, 2), col // 2
    chips = n_col // 2
    rows = x_ref.shape[0]
    half_n = n_row // 2
    side = (row >= half_n).astype(jnp.int32)
    other = 1 - side
    place = jnp.where(side == 0, row, n_row - 1 - row)
    inner = jnp.where(side == 0, row + 1, row - 1)
    outer = jnp.where(side == 0, jnp.maximum(row - 1, 0), jnp.minimum(row + 1, n_row - 1))
    has_out = place > 0
    is_mid = place == half_n - 1

    def weight_in(c):
        return pltpu.make_async_copy(
            win_ref.at[:, pl.ds(pl.multiple_of(c * fc, fc), fc)], wi.at[c], w_sem.at[0, c]
        )

    def weight_out(c):
        return pltpu.make_async_copy(
            wout_ref.at[pl.ds(pl.multiple_of(c * fc, fc), fc), :], wo.at[c], w_sem.at[1, c]
        )

    def mine(k):
        src, dst = ((x_ref, xf), (g_ref, gf))[k]
        return pltpu.make_async_copy(src, dst.at[pl.ds(pl.multiple_of(col * rows, rows), rows), :], own_sem.at[k])

    for k in range(2):
        mine(k).start()

    def fetch(c, carry):
        weight_in(c).start()
        weight_out(c).start()
        return carry

    lax.fori_loop(0, nch, fetch, 0)

    barrier = pltpu.get_barrier_semaphore()
    for q in range(1, chips):
        pl.semaphore_signal(
            barrier, inc=1, device_id={"col": lax.rem(chip + q, chips) * 2 + core}, device_id_type=MESH
        )
    pl.semaphore_signal(barrier, inc=1, device_id={"col": chip * 2 + 1 - core}, device_id_type=MESH)
    pl.semaphore_signal(barrier, inc=1, device_id={"row": inner}, device_id_type=MESH)

    @pl.when(has_out)
    def _():
        pl.semaphore_signal(barrier, inc=1, device_id={"row": outer}, device_id_type=MESH)

    pl.semaphore_wait(barrier, chips + 1 + has_out.astype(jnp.int32))

    def block(k, owner):
        return (xf, gf)[k].at[pl.ds(pl.multiple_of(owner * rows, rows), rows), :]

    def far(k, q):
        return pltpu.make_async_remote_copy(
            src_ref=(x_ref, g_ref)[k],
            dst_ref=block(k, col),
            send_sem=ag_send.at[k, q],
            recv_sem=ag_recv.at[k, col],
            device_id={"col": lax.rem(chip + q, chips) * 2 + core},
            device_id_type=MESH,
        )

    def near(k, q):
        owner = lax.rem(chip + chips - q, chips) * 2 + core
        return pltpu.make_async_remote_copy(
            src_ref=x_ref if (q == 0 and k == 0) else g_ref if q == 0 else block(k, owner),
            dst_ref=block(k, owner),
            send_sem=ag_send.at[k, chips + q],
            recv_sem=ag_recv.at[k, owner],
            device_id={"col": chip * 2 + 1 - core},
            device_id_type=MESH,
        )

    def landed(k, owner):
        return pltpu.make_async_remote_copy(
            src_ref=block(k, owner),
            dst_ref=block(k, owner),
            send_sem=ag_send.at[k, 0],
            recv_sem=ag_recv.at[k, owner],
            device_id={"col": chip * 2 + 1 - core},
            device_id_type=MESH,
        )

    def pass_on(k):
        mine(k).wait()
        for q in range(1, chips):
            landed(k, lax.rem(chip + chips - q, chips) * 2 + core).wait_recv()
            near(k, q).start()

    def arrived(k):
        for q in range(chips):
            landed(k, lax.rem(chip + chips - q, chips) * 2 + 1 - core).wait_recv()
        pltpu.make_async_copy((xf, gf)[k], (x_out, g_out)[k], out_sem.at[k]).start()

    def begin(k):
        for q in range(1, chips):
            far(k, q).start()
        near(k, 0).start()

    begin(0)
    pass_on(0)
    begin(1)
    gi[...] = jnp.zeros_like(gi)
    arrived(0)

    def send_sum(c, k):
        return pltpu.make_async_remote_copy(
            src_ref=s.at[k, c], dst_ref=r.at[k, c], send_sem=s_send.at[k, c], recv_sem=s_recv.at[k, c],
            device_id={"row": inner}, device_id_type=MESH,
        )

    def swap_sum(c, k):
        return pltpu.make_async_remote_copy(
            src_ref=s.at[k, c, other], dst_ref=e.at[k, c], send_sem=e_send.at[k, c], recv_sem=e_recv.at[k, c],
            device_id={"row": inner}, device_id_type=MESH,
        )

    def send_hidden(c, half, target, way):
        return pltpu.make_async_remote_copy(
            src_ref=hb.at[c, half], dst_ref=hb.at[c, half],
            send_sem=h_send.at[c, half, way], recv_sem=h_recv.at[c, half],
            device_id={"row": target}, device_id_type=MESH,
        )

    def save_hidden(c):
        return pltpu.make_async_copy(hb.at[c], h_out.at[c], out_sem.at[3 + c])

    tokens = xf.shape[0]
    split = tokens // 2

    def pre_terms(c):
        weight_in(c).wait()
        return jnp.dot(xf[...], wi[c], preferred_element_type=f32).reshape(2, split, fc)

    ahead = early.shape[0]

    def work_ahead(c, carry):
        early[c] = pre_terms(c)
        return carry

    def local_sum(c, k):
        if k == 0:
            @pl.when(c < ahead)
            def _():
                pf[0] = early[jnp.minimum(c, ahead - 1)]

            @pl.when(c >= ahead)
            def _():
                pf[0] = pre_terms(c)

        else:
            weight_out(c).wait()
            pf[1] = nt_dot(gf[...], wo[c]).reshape(2, split, fc)

        @pl.when(has_out)
        def _():
            send_sum(c, k).wait_recv()
            pf[k] += r[k, c].astype(f32)

    def input_terms(c):
        save_hidden(c).start()
        grads = hb[c, :, 1].reshape(tokens, fc)
        for at in range(0, gi.shape[1], fc):
            gi[:, at : at + fc] += nt_dot(grads, wi[c, at : at + fc, :])

    @pl.when(jnp.logical_not(is_mid))
    def _():
        def inwards(k, c, carry):
            local_sum(c, k)
            s[k, c] = pf[k].astype(bf16)
            send_sum(c, k).start()
            return carry

        def inwards_ahead(c, carry):
            work_ahead(c, carry)
            return inwards(0, c, carry)

        lax.fori_loop(0, ahead, inwards_ahead, 0)
        pass_on(1)
        arrived(1)
        lax.fori_loop(0, ahead, functools.partial(inwards, 1), 0)

        def inwards_both(c, carry):
            return inwards(1, c, inwards(0, c, carry))

        lax.fori_loop(ahead, nch, inwards_both, 0)

        def outwards(c, carry):
            for half in range(2):
                send_hidden(c, half, inner, 0).wait_recv()

                @pl.when(has_out)
                def _():
                    send_hidden(c, half, outer, 1).start()

            input_terms(c)
            return carry

        lax.fori_loop(0, nch, outwards, 0)

        def drain(c, carry):
            for k in range(2):
                send_sum(c, k).wait_send()

            @pl.when(has_out)
            def _():
                for half in range(2):
                    send_hidden(c, half, outer, 1).wait_send()

            return carry

        lax.fori_loop(0, nch, drain, 0)

    @pl.when(is_mid)
    def _():
        lax.fori_loop(0, ahead, work_ahead, 0)
        pass_on(1)
        arrived(1)

        def tick(t, carry):
            @pl.when(t < nch)
            def _():
                for k in range(2):
                    local_sum(t, k)
                    s[k, t, other] = pf[k, other].astype(bf16)
                    swap_sum(t, k).start()
                    keep[lax.rem(t, 2), k] = pf[k, side]

            @pl.when((t >= 1) & (t <= nch))
            def _():
                c = t - 1
                sums = []
                for k in range(2):
                    swap_sum(c, k).wait_recv()
                    sums.append(keep[lax.rem(c, 2), k] + e[k, c].astype(f32))
                hidden, hid_grad = gelu_pair(*sums)
                hb[c, side, 0] = hidden
                hb[c, side, 1] = hid_grad
                send_hidden(c, side, inner, 0).start()

                @pl.when(has_out)
                def _():
                    send_hidden(c, side, outer, 1).start()

            @pl.when(t >= 2)
            def _():
                c = t - 2
                send_hidden(c, other, inner, 0).wait_recv()

                @pl.when(has_out)
                def _():
                    send_hidden(c, other, outer, 1).start()

                input_terms(c)

            return carry

        lax.fori_loop(0, nch + 2, tick, 0)

        def drain(c, carry):
            for k in range(2):
                swap_sum(c, k).wait_send()
            send_hidden(c, side, inner, 0).wait_send()

            @pl.when(has_out)
            def _():
                send_hidden(c, side, outer, 1).wait_send()
                send_hidden(c, other, outer, 1).wait_send()

            return carry

        lax.fori_loop(0, nch, drain, 0)

    def own(chip_to, core_to):
        return pl.ds(pl.multiple_of((chip_to * 2 + core_to) * rows, rows), rows)

    def to_core(q):
        target = lax.rem(chip + q, chips)
        return pltpu.make_async_remote_copy(
            src_ref=gi.at[own(target, 1 - core), :], dst_ref=pair.at[q],
            send_sem=pair_send.at[q], recv_sem=pair_recv.at[q],
            device_id={"col": chip * 2 + 1 - core}, device_id_type=MESH,
        )

    def hand_out(q):
        if q == 0:
            return pltpu.make_async_copy(pair.at[0], own_out, part_sem.at[0])
        return pltpu.make_async_copy(part.at[q], part_out[q - 1], part_sem.at[q])

    for q in range(chips - 1, -1, -1):
        to_core(q).start()
    for q in range(chips - 1, -1, -1):
        to_core(q).wait_recv()
        both = gi[own(lax.rem(chip + q, chips), core), :] + pair[q]
        if q == 0:
            pair[0] = both
        else:
            part[q] = both.astype(bf16)
        hand_out(q).start()
    for q in range(chips):
        to_core(q).wait_send()
        hand_out(q).wait()
    for k in range(2):
        for q in range(1, chips):
            far(k, q).wait_send()
        for q in range(chips):
            near(k, q).wait_send()
    pltpu.make_async_copy(xf, x_out, out_sem.at[0]).wait()
    pltpu.make_async_copy(gf, g_out, out_sem.at[1]).wait()

    def saved(c, carry):
        save_hidden(c).wait()
        return carry

    lax.fori_loop(0, nch, saved, 0)


def weights_kernel(nch, fc, wide, x_ref, g_ref, hid_ref, all_ref, gwi_ref, gwo_ref, slots_in, slots_out, sems):
    tokens = g_ref.shape[0]
    step = pl.program_id(0)
    depth = slots_in.shape[0]
    slot = lax.rem(step, depth)

    def write_out(i, s):
        rows = pl.ds(pl.multiple_of(i * fc, fc), fc)
        return pltpu.make_async_copy(slots_out.at[s], gwo_ref.at[rows, :], sems.at[0, s])

    def write_in(i, s):
        rows = pl.ds(pl.multiple_of(i * wide, wide), wide)
        return pltpu.make_async_copy(slots_in.at[s], gwi_ref.at[rows, :], sems.at[1, s])

    @pl.when(step >= depth)
    def _():
        write_out(step - depth, slot).wait()

    turned = hid_ref[0, :, 0].reshape(tokens, fc).T
    for at in range(0, g_ref.shape[1], fc):
        slots_out[slot, :, at : at + fc] = jnp.dot(
            turned, g_ref[:, at : at + fc], preferred_element_type=f32
        ).astype(bf16)
    write_out(step, slot).start()

    @pl.when(step >= depth)
    def _():
        write_in(step - depth, slot).wait()

    turned = x_ref[...].T
    for c in range(nch):
        grads = all_ref[c, :, 1].reshape(tokens, fc)
        slots_in[slot, :, c * fc : (c + 1) * fc] = jnp.dot(
            turned, grads, preferred_element_type=f32
        ).astype(bf16)
    write_in(step, slot).start()

    @pl.when(step == nch - 1)
    def _():
        for i in range(nch - depth, nch):
            write_out(i, i % depth).wait()
            write_in(i, i % depth).wait()


def on_device(n_row, n_col, inputs, out_grad, weight_in, weight_out):
    rows, d = inputs.shape
    f = weight_in.shape[1]
    tokens = rows * n_col
    fc = 256 if f % 256 == 0 else 128
    nch = f // fc
    split = tokens // 2
    chips = n_col // 2
    any_spec = pl.BlockSpec(memory_space=pl.ANY)
    dma = pltpu.SemaphoreType.DMA
    hid, full_in, full_grad, own, *parts = pl.pallas_call(
        functools.partial(exchange_kernel, n_row, n_col, nch, fc),
        out_shape=(
            jax.ShapeDtypeStruct((nch, 2, 2, split, fc), bf16),
            jax.ShapeDtypeStruct((tokens, d), bf16),
            jax.ShapeDtypeStruct((tokens, d), bf16),
            jax.ShapeDtypeStruct((rows, d), f32),
        )
        + (jax.ShapeDtypeStruct((rows, d), bf16),) * (chips - 1),
        in_specs=[any_spec] * 4,
        out_specs=(any_spec,) * (3 + chips),
        scratch_shapes=[
            pltpu.VMEM((tokens, d), bf16),
            pltpu.VMEM((tokens, d), bf16),
            pltpu.VMEM((nch, d, fc), bf16),
            pltpu.VMEM((nch, fc, d), bf16),
            pltpu.VMEM((2, nch, 2, split, fc), bf16),
            pltpu.VMEM((2, nch, 2, split, fc), bf16),
            pltpu.VMEM((2, nch, split, fc), bf16),
            pltpu.VMEM((nch, 2, 2, split, fc), bf16),
            pltpu.VMEM((2, 2, split, fc), f32),
            pltpu.VMEM((2, 2, split, fc), f32),
            pltpu.VMEM((min(4, nch), 2, split, fc), f32),
            pltpu.VMEM((tokens, d), f32),
            pltpu.VMEM((chips, rows, d), f32),
            pltpu.VMEM((chips, rows, d), bf16),
            dma((2, nch)),
            dma((2, n_col)),
            dma((2, n_col)),
            dma((2,)),
            dma((2, nch)),
            dma((2, nch)),
            dma((2, nch)),
            dma((2, nch)),
            dma((nch, 2, 2)),
            dma((nch, 2)),
            dma((3 + nch,)),
            dma((chips,)),
            dma((chips,)),
            dma((chips,)),
        ],
        compiler_params=pltpu.CompilerParams(
            collective_id=0, has_side_effects=True, vmem_limit_bytes=56 * 2**20
        ),
        cost_estimate=pl.CostEstimate(
            flops=6 * tokens * d * f, bytes_accessed=4 * d * f, transcendentals=tokens * f
        ),
        name="exchange",
    )(inputs, out_grad, weight_in, weight_out)

    moved = [
        lax.ppermute(
            term, "col", [(c, ((c // 2 + q) % chips) * 2 + c % 2) for c in range(n_col)]
        )
        for q, term in enumerate(parts, 1)
    ]
    wide = fc if d % nch else d // nch
    steps = nch
    depth = min(4, nch)
    grad_weight_in, grad_weight_out = pl.pallas_call(
        functools.partial(weights_kernel, nch, fc, wide),
        grid=(steps,),
        out_shape=(jax.ShapeDtypeStruct((d, f), bf16), jax.ShapeDtypeStruct((f, d), bf16)),
        in_specs=[
            pl.BlockSpec((tokens, wide), lambda i: (0, i)),
            pl.BlockSpec((tokens, d), lambda i: (0, 0)),
            pl.BlockSpec((1, 2, 2, split, fc), lambda i: (i, 0, 0, 0, 0)),
            pl.BlockSpec((nch, 2, 2, split, fc), lambda i: (0, 0, 0, 0, 0)),
        ],
        out_specs=(any_spec, any_spec),
        scratch_shapes=[
            pltpu.VMEM((depth, wide, f), bf16),
            pltpu.VMEM((depth, fc, d), bf16),
            dma((2, depth)),
        ],
        compiler_params=pltpu.CompilerParams(vmem_limit_bytes=60 * 2**20),
        cost_estimate=pl.CostEstimate(
            flops=4 * tokens * d * f, bytes_accessed=4 * d * f, transcendentals=0
        ),
        name="weight_grads",
    )(full_in, full_grad, hid, hid)
    total = own
    for term in moved:
        total = total + term.astype(f32)
    return (total.astype(bf16), grad_weight_in, grad_weight_out)


def solution(mesh):
    placed = (P("col", "row"), P("col", "row"), P("row", "col"), P("col", "row"))
    return jax.shard_map(
        functools.partial(on_device, mesh.shape["row"], mesh.shape["col"]),
        mesh=mesh,
        in_specs=placed,
        out_specs=(P("col", "row"), P("row", "col"), P("col", "row")),
        check_vma=False,
    )
```
